32 devices in a mesh: parts: 1, wide: 16 (over z, y, x), narrow: 2 (over core).
Axes of the slice: x: 2, y: 2, z: 4, core: 2. Of those that a mesh axis runs over, the one named last changes fastest.
Arguments:
- tokens: bfloat16 [4096, 3584], P(('parts', 'wide', 'narrow')), may hold values from -6 to 6
- grad_out: bfloat16 [4096, 3584], P(('parts', 'wide', 'narrow')), may hold values from -6 to 6
- expert_ids: int32 [4096], P(('parts', 'wide', 'narrow')), may hold values from 0 to 7, as said below
- combine: float32 [4096], P(('parts', 'wide', 'narrow')), may hold values from 0.1 to 1
- w_gate: bfloat16 [2, 3584, 4096], P('narrow', None, 'wide'), may hold values from -0.09375 to 0.09375
- w_up: bfloat16 [2, 3584, 4096], P('narrow', None, 'wide'), may hold values from -0.09375 to 0.09375
- w_down: bfloat16 [2, 4096, 3584], P('narrow', 'wide'), may hold values from -0.1875 to 0.1875
Outputs:
- token_grad: bfloat16 [4096, 3584], P(('parts', 'wide', 'narrow'))
- prob_grad: float32 [4096], P(('parts', 'wide', 'narrow'))
The draws below stay inside these ranges and needn't reach their ends.
Inputs may be any that keep to these rules, and one draw needn't show every extreme that they name: `expert_ids`: among the 128 tokens of each device, every expert is chosen at most 32 times; one expert, the same for all devices, is chosen exactly 32 times on every device.
All inputs are finite; a program needn't handle non-finite values.
Results may differ from the reference program's by a relative error of at most 0.0051.
Values may be sent and summed in bfloat16 or wider, within the bound.
No kernel may reach another device: no remote copies, remote signals or barrier semaphores. Data moves between devices by JAX's collectives and lax.ppermute only.
A program may use at most 128 MiB of HBM per device.

```python
import math
import jax
import jax.numpy as jnp
from jax import lax

D = 3584
F = 1024
TOK_DEV = 128
BLOCKS = 4
EXPERTS = 8
CAP = 32
TOKENS = 4096
N_NARROW = 2


def draw_expert_ids(key, part):
    key = jax.random.fold_in(key, 11)
    hot_key, rank_key, box_key = jax.random.split(key, 3)
    hot = jax.random.randint(hot_key, (), 0, EXPERTS)
    blocks = TOKENS // TOK_DEV
    boxes = (EXPERTS - 1) * CAP
    ranks = jax.vmap(lambda k: jax.random.permutation(k, TOK_DEV))(jax.random.split(rank_key, blocks))
    fills = jax.vmap(lambda k: jax.random.permutation(k, boxes))(jax.random.split(box_key, blocks))
    picked = jnp.take_along_axis(fills, jnp.clip(ranks - CAP, 0, boxes - 1), axis=1)
    others = (hot + 1 + picked // CAP) % EXPERTS
    chosen = jnp.where(ranks < CAP, hot, others)
    return chosen.reshape(TOKENS).astype(jnp.int32)


def shard_levels(key, extent, cuts, least, high):
    def one(axis_at, blocks):
        draws = jax.random.uniform(jax.random.fold_in(jax.random.fold_in(key, 6), axis_at), (blocks,), jnp.float32, least / len(cuts), high / len(cuts))
        return jnp.repeat(jnp.exp(draws), extent[axis_at] // blocks).reshape((-1,) + (1,) * (len(extent) - axis_at - 1))

    loudness = one(*cuts[0])
    for cut in cuts[1:]:
        loudness = loudness * one(*cut)
    return loudness


def centred(rng, dims, deviation, most, shards=(), held_as=jnp.bfloat16):
    array = deviation * jax.random.normal(rng, dims, jnp.float32)
    if shards:
        array = array * shard_levels(rng, dims, shards, -0.22, 0.18)
    return jnp.clip(array, -most, most).astype(held_as)


def setup_inputs(seed: int = 0, part: int = 0) -> dict:
    key_list = jax.random.split(jax.random.key(seed), 8)
    part_splits = jax.random.split(jax.random.fold_in(key_list[7], part), 8)
    return {
        "tokens": centred(part_splits[0], (TOKENS, D), 1.0, 6.0, ((0, 32),)),
        "grad_out": centred(part_splits[1], (TOKENS, D), 1.0, 6.0, ((0, 32),)),
        "expert_ids": draw_expert_ids(jax.random.fold_in(jax.random.fold_in(key_list[7], part), 71), part),
        "combine": jnp.clip(jnp.exp(math.log(1.0) - 2.3025851 * jax.random.uniform(part_splits[3], (TOKENS,), jnp.float32) ** shard_levels(part_splits[3], (TOKENS,), ((0, 32),), -0.2, 0.2)), 0.1, 1.0),
        "w_gate": centred(key_list[4], (N_NARROW, D, BLOCKS * F), D ** -0.5, 0.09375, ((0, 2), (2, 16))),
        "w_up": centred(key_list[5], (N_NARROW, D, BLOCKS * F), D ** -0.5, 0.09375, ((0, 2), (2, 16))),
        "w_down": centred(key_list[6], (N_NARROW, BLOCKS * F, D), F ** -0.5, 0.1875, ((0, 2), (1, 16))),
    }


def silu_parts(gate):
    sigma = jax.nn.sigmoid(gate)
    return gate * sigma, sigma * (1.0 + gate * (1.0 - sigma))


def reference(tokens, grad_out, expert_ids, combine, w_gate, w_up, w_down):
    sources = TOKENS // TOK_DEV
    columns = sources * CAP
    blocked = expert_ids.reshape(sources, TOK_DEV)
    hits = (blocked[:, :, None] == jnp.arange(EXPERTS, dtype=jnp.int32)[None, None, :]).astype(jnp.int32)
    slot = jnp.sum((jnp.cumsum(hits, axis=1) - hits) * hits, axis=2).reshape(TOKENS).astype(jnp.int32)
    anchor = (jnp.arange(TOKENS, dtype=jnp.int32) // TOK_DEV).astype(jnp.int32)
    place = (anchor * CAP + slot).astype(jnp.int32)
    table = jnp.full((EXPERTS, columns), TOKENS, jnp.int32)
    table = table.at[expert_ids, place].set(jnp.arange(TOKENS, dtype=jnp.int32))
    x_padded = jnp.concatenate([tokens, jnp.zeros((1, D), tokens.dtype)], axis=0)
    g_padded = jnp.concatenate([grad_out, jnp.zeros((1, D), grad_out.dtype)], axis=0)
    gate_all = w_gate.reshape(N_NARROW, D, BLOCKS, F).transpose(0, 2, 1, 3).reshape(EXPERTS, D, F)
    up_all = w_up.reshape(N_NARROW, D, BLOCKS, F).transpose(0, 2, 1, 3).reshape(EXPERTS, D, F)
    down_all = w_down.reshape(EXPERTS, F, D)

    def one_expert(item):
        rows, gate_w, up_w, down_w = item
        rows_x = x_padded[rows]
        rows_g = g_padded[rows]
        gate = jnp.dot(rows_x, gate_w, preferred_element_type=jnp.float32)
        up = jnp.dot(rows_x, up_w, preferred_element_type=jnp.float32)
        back = jnp.dot(rows_g, down_w.T, preferred_element_type=jnp.float32)
        act, slope = silu_parts(gate)
        prob_part = jnp.sum(act * up * back, axis=1)
        gate_grad = (back * up * slope).astype(jnp.bfloat16)
        up_grad = (back * act).astype(jnp.bfloat16)
        input_part = jnp.dot(gate_grad, gate_w.T, preferred_element_type=jnp.float32)
        input_part = input_part + jnp.dot(up_grad, up_w.T, preferred_element_type=jnp.float32)
        return input_part, prob_part

    parts, probs = lax.map(one_expert, (table, gate_all, up_all, down_all))
    token_grad = (combine[:, None] * parts[expert_ids, place]).astype(jnp.bfloat16)
    prob_grad = probs[expert_ids, place]
    return token_grad, prob_grad
```

```python
import jax
import jax.numpy as jnp
from jax import lax
from jax.sharding import PartitionSpec as P

SHARDS = 4
AXES = ("wide", "narrow")


def silu_parts(gate):
    sigma = jax.nn.sigmoid(gate)
    return (gate * sigma, sigma * (1.0 + gate * (1.0 - sigma)))


def times(left, right):
    return jnp.dot(left, right, preferred_element_type=jnp.float32)


def times_transposed(left, right):
    return lax.dot_general(
        left, right, (((1,), (1,)), ((), ())), preferred_element_type=jnp.float32
    )


def shards(tokens, grad_out, expert_ids, combine, w_gate, w_up, w_down):
    wide = lax.axis_size("wide")
    narrow = lax.axis_size("narrow")
    blocks = wide // SHARDS
    experts = blocks * narrow
    count, width = tokens.shape
    cap = 2 * count // experts
    block = lax.axis_index("wide") // SHARDS
    core = lax.axis_index("narrow")

    def permute(value, target):
        pairs = []
        for w in range(wide):
            for c in range(narrow):
                b, s, n = target(w // SHARDS, w % SHARDS, c)
                pairs.append((w * narrow + c, (b * SHARDS + s) * narrow + n))
        return lax.ppermute(value, AXES, pairs)

    def swap_weights(value):
        return permute(value, lambda b, s, c: (b, s ^ (1 if c == 0 else 2), c))

    def swap_rows(value):
        return permute(value, lambda b, s, c: (b, s ^ (2 if c == 0 else 1), c))

    def send(value, k, m):
        if k == 0 and m == 0:
            return value
        return permute(value, lambda b, s, c: ((b + k) % blocks, s, (c + m) % narrow))

    def give_back(value, k, m):
        if k == 0 and m == 0:
            return value
        return permute(value, lambda b, s, c: ((b - k) % blocks, s, (c - m) % narrow))

    gate_w = jnp.concatenate([w_gate[0], swap_weights(w_gate[0])], axis=1)
    up_w = jnp.concatenate([w_up[0], swap_weights(w_up[0])], axis=1)
    down_w = jnp.concatenate([w_down[0], swap_weights(w_down[0])], axis=0)

    hits = (expert_ids[:, None] == jnp.arange(experts, dtype=jnp.int32)[None, :]).astype(
        jnp.float32
    )
    earlier = (jnp.arange(count)[:, None] > jnp.arange(count)[None, :]).astype(jnp.float32)
    before = jnp.dot(earlier, hits, precision=lax.Precision.HIGHEST)
    slot = jnp.sum(before * hits, axis=1).astype(jnp.int32)
    shift = (expert_ids % blocks - block + blocks) % blocks
    turn = (expert_ids // blocks - core + narrow) % narrow
    place = (shift * narrow + turn) * cap + slot
    select = jnp.arange(experts * cap, dtype=jnp.int32)[:, None] == place[None, :]
    packed_x = times(select.astype(jnp.bfloat16), tokens).astype(jnp.bfloat16)
    packed_g = times(select.astype(jnp.bfloat16), grad_out).astype(jnp.bfloat16)
    packed = jnp.stack(
        [packed_x.reshape(experts, cap, width), packed_g.reshape(experts, cap, width)], axis=1
    )

    order = sorted(range(blocks), key=lambda k: (k != 0, -min(k, blocks - k), k))
    rows = {}
    for k in order:
        own = [send(packed[k * narrow + m], k, m) for m in range(narrow)]
        other = [swap_rows(part) for part in own]
        rows[k] = (own, other)

    back_rows = {}
    back_probs = {}
    half = narrow * cap
    for k in order:
        own, other = rows[k]
        x = jnp.concatenate([part[0] for part in own + other], axis=0)
        g = jnp.concatenate([part[1] for part in own + other], axis=0)
        gate = times(x, gate_w)
        up = times(x, up_w)
        back = times_transposed(g, down_w)
        act, slope = silu_parts(gate)
        prob_part = jnp.sum(act * up * back, axis=1)
        gate_grad = (back * up * slope).astype(jnp.bfloat16)
        up_grad = (back * act).astype(jnp.bfloat16)
        partial = times_transposed(gate_grad, gate_w) + times_transposed(up_grad, up_w)
        mine = partial[:half] + swap_rows(partial[half:].astype(jnp.bfloat16)).astype(jnp.float32)
        mine = mine.astype(jnp.bfloat16)
        prob = prob_part[:half] + swap_rows(prob_part[half:])
        for m in range(narrow):
            back_rows[k * narrow + m] = give_back(mine[m * cap : (m + 1) * cap], k, m)
            back_probs[k * narrow + m] = give_back(prob[m * cap : (m + 1) * cap], k, m)

    returned = jnp.concatenate([back_rows[i] for i in range(experts)], axis=0)
    probs = jnp.concatenate([back_probs[i] for i in range(experts)], axis=0)
    token_grad = combine[:, None] * times(select.T.astype(jnp.bfloat16), returned)
    prob_grad = jnp.sum(jnp.where(select, probs[:, None], 0.0), axis=0)
    return (token_grad.astype(jnp.bfloat16), prob_grad)


def solution(mesh):
    in_specs = (
        P(("parts", "wide", "narrow"), None),
        P(("parts", "wide", "narrow"), None),
        P(("parts", "wide", "narrow")),
        P(("parts", "wide", "narrow")),
        P("narrow", None, "wide"),
        P("narrow", None, "wide"),
        P("narrow", "wide", None),
    )
    out_specs = (P(("parts", "wide", "narrow"), None), P(("parts", "wide", "narrow")))
    return jax.shard_map(shards, mesh=mesh, in_specs=in_specs, out_specs=out_specs, check_vma=False)
```

```python
import jax
import jax.numpy as jnp
from jax import lax
from jax.sharding import PartitionSpec as P

SHARDS = 4
LANES = 128
AXES = ("wide", "narrow")


def silu_parts(gate):
    sigma = jax.nn.sigmoid(gate)
    return (gate * sigma, sigma * (1.0 + gate * (1.0 - sigma)))


def times(left, right):
    return jnp.dot(left, right, preferred_element_type=jnp.float32)


def times_transposed(left, right):
    return lax.dot_general(
        left, right, (((1,), (1,)), ((), ())), preferred_element_type=jnp.float32
    )


def tie(value, *before):
    return lax.optimization_barrier((value,) + before)[0]


def with_prob(rows, prob):
    high = lax.reduce_precision(prob, 8, 7)
    column = lax.broadcasted_iota(jnp.int32, (prob.shape[0], LANES), 1)
    tail = jnp.where(
        column == 0, high[:, None], jnp.where(column == 1, (prob - high)[:, None], 0.0)
    )
    return jnp.concatenate([rows.astype(jnp.bfloat16), tail.astype(jnp.bfloat16)], axis=1)


def shards(tokens, grad_out, expert_ids, combine, w_gate, w_up, w_down):
    wide = lax.axis_size("wide")
    narrow = lax.axis_size("narrow")
    blocks = wide // SHARDS
    experts = blocks * narrow
    count, width = tokens.shape
    cap = 2 * count // experts
    half = narrow * cap
    block = lax.axis_index("wide") // SHARDS
    core = lax.axis_index("narrow")

    def permute(value, target):
        pairs = []
        for w in range(wide):
            for c in range(narrow):
                b, s, n = target(w // SHARDS, w % SHARDS, c)
                pairs.append((w * narrow + c, (b * SHARDS + s) * narrow + n))
        return lax.ppermute(value, AXES, pairs)

    def swap_weights(value):
        return permute(value, lambda b, s, c: (b, s ^ (1 if c == 0 else 2), c))

    def swap_rows(value):
        return permute(value, lambda b, s, c: (b, s ^ (2 if c == 0 else 1), c))

    def send(value, k, m):
        return permute(value, lambda b, s, c: (b ^ k, s, (c + m) % narrow))

    def give_back(value, k, m):
        if k == 0 and m == 0:
            return value
        return permute(value, lambda b, s, c: (b ^ k, s, (c - m) % narrow))

    both_w = jnp.concatenate([w_gate[0], w_up[0]], axis=1)
    both_in = swap_weights(both_w)
    down_in = swap_weights(w_down[0])
    units = w_gate.shape[2]

    order = [blocks // 2] + [k for k in range(1, blocks) if k != blocks // 2] + [0]
    token = jnp.arange(count, dtype=jnp.int32)
    twins = (expert_ids[:, None] == expert_ids[None, :]) & (token[:, None] < token[None, :])
    slot = jnp.sum(twins.astype(jnp.int32), axis=0)
    shift = (expert_ids % blocks) ^ block
    position = sum(i * (shift == k).astype(jnp.int32) for i, k in enumerate(order))
    turn = (expert_ids // blocks - core + narrow) % narrow
    place = (position * narrow + turn) * cap + slot
    select = jnp.arange(experts * cap, dtype=jnp.int32)[:, None] == place[None, :]
    packed_x = times(select.astype(jnp.bfloat16), tokens).astype(jnp.bfloat16)
    packed_g = times(select.astype(jnp.bfloat16), grad_out).astype(jnp.bfloat16)
    packed = jnp.stack(
        [
            packed_x.reshape(blocks, narrow, cap, width),
            packed_g.reshape(blocks, narrow, cap, width),
        ],
        axis=2,
    )

    turned = [
        permute(packed[:, m], lambda b, s, c: (b, s, (c + m) % narrow)) for m in range(1, narrow)
    ]
    merged = jnp.stack([packed[:, 0]] + turned, axis=1)
    arrived = []
    for i, k in enumerate(order):
        if k == 0:
            arrived.append(merged[i])
        else:
            chunk = merged[i] if i < 2 else tie(merged[i], arrived[i - 2])
            arrived.append(send(chunk, k, 0))

    swapped = [None] * blocks

    def swap_in(i, *wait):
        swapped[i] = swap_rows(tie(arrived[i], *wait))

    def compute(i, *wait):
        mine, other = arrived[i], tie(swapped[i], *wait)
        x = jnp.concatenate([mine[:, 0].reshape(half, width), other[:, 0].reshape(half, width)])
        g = jnp.concatenate([mine[:, 1].reshape(half, width), other[:, 1].reshape(half, width)])
        partial, prob = 0.0, 0.0
        for forward_w, down_w in ((both_w, w_down[0]), (both_in, down_in)):
            forward = times(x, forward_w)
            gate, up = forward[:, :units], forward[:, units:]
            back = times_transposed(g, down_w)
            act, slope = silu_parts(gate)
            prob = prob + jnp.sum(act * up * back, axis=1)
            grads = jnp.concatenate([back * up * slope, back * act], axis=1).astype(jnp.bfloat16)
            partial = partial + times_transposed(grads, forward_w)
        theirs = with_prob(partial[half:], prob[half:])
        return partial[:half], prob[:half], theirs

    def finish(i, part, *wait):
        partial, prob, theirs = part
        theirs = tie(swap_rows(theirs), *wait).astype(jnp.float32)
        total = with_prob(
            partial + theirs[:, :width], prob + (theirs[:, width] + theirs[:, width + 1])
        )
        return total

    parts = [None] * blocks
    totals = [None] * blocks
    swap_in(0)
    swap_in(1)
    for first in range(0, blocks, 2):
        last = min(first + 1, blocks - 1)
        for i in range(first, last + 1):
            wait = [parts[i - 1][2]] if i > first else []
            if i == first and i > 0:
                wait.append(totals[i - 1])
            parts[i] = compute(i, *wait)
            if i == first:
                for j in range(last + 1, min(last + 3, blocks)):
                    swap_in(j, parts[i][2], arrived[min(last + 1, blocks - 1)])
        for i in range(first, last + 1):
            totals[i] = finish(i, parts[i], parts[last][2])

    rows = 0.0
    select = select.T.reshape(count, blocks, half).astype(jnp.bfloat16)
    for i in range(blocks):
        total = totals[i] if order[i] == 0 else give_back(totals[i], order[i], 0)
        parts_in = [total[:cap]]
        for m in range(1, narrow):
            parts_in.append(give_back(total[m * cap : (m + 1) * cap], 0, m))
        rows = rows + times(select[:, i], jnp.concatenate(parts_in, axis=0))
    token_grad = (combine[:, None] * rows[:, :width]).astype(jnp.bfloat16)
    prob_grad = rows[:, width] + rows[:, width + 1]
    return (token_grad, prob_grad)


def solution(mesh):
    in_specs = (
        P(("parts", "wide", "narrow"), None),
        P(("parts", "wide", "narrow"), None),
        P(("parts", "wide", "narrow")),
        P(("parts", "wide", "narrow")),
        P("narrow", None, "wide"),
        P("narrow", None, "wide"),
        P("narrow", "wide", None),
    )
    out_specs = (P(("parts", "wide", "narrow"), None), P(("parts", "wide", "narrow")))
    return jax.shard_map(shards, mesh=mesh, in_specs=in_specs, out_specs=out_specs, check_vma=False)
```

```python
import jax
import jax.numpy as jnp
from jax import lax
from jax.sharding import PartitionSpec as P

SHARDS = 4
LANES = 128
AXES = ("wide", "narrow")


def silu_parts(gate):
    sigma = jax.nn.sigmoid(gate)
    return (gate * sigma, sigma * (1.0 + gate * (1.0 - sigma)))


def times(left, right):
    return jnp.dot(left, right, preferred_element_type=jnp.float32)


def times_transposed(left, right):
    return lax.dot_general(
        left, right, (((1,), (1,)), ((), ())), preferred_element_type=jnp.float32
    )


def tie(value, *before):
    return lax.optimization_barrier((value,) + before)[0]


def with_prob(rows, prob):
    high = lax.reduce_precision(prob, 8, 7)
    column = lax.broadcasted_iota(jnp.int32, (prob.shape[0], LANES), 1)
    tail = jnp.where(
        column == 0, high[:, None], jnp.where(column == 1, (prob - high)[:, None], 0.0)
    )
    return jnp.concatenate([rows.astype(jnp.bfloat16), tail.astype(jnp.bfloat16)], axis=1)


def shards(tokens, grad_out, expert_ids, combine, w_gate, w_up, w_down):
    wide = lax.axis_size("wide")
    narrow = lax.axis_size("narrow")
    blocks = wide // SHARDS
    experts = blocks * narrow
    count, width = tokens.shape
    cap = 2 * count // experts
    half = narrow * cap
    block = lax.axis_index("wide") // SHARDS
    core = lax.axis_index("narrow")

    def permute(value, target):
        pairs = []
        for w in range(wide):
            for c in range(narrow):
                b, s, n = target(w // SHARDS, w % SHARDS, c)
                pairs.append((w * narrow + c, (b * SHARDS + s) * narrow + n))
        return lax.ppermute(value, AXES, pairs)

    def swap_weights(value):
        return permute(value, lambda b, s, c: (b, s ^ (1 if c == 0 else 2), c))

    def swap_rows(value):
        return permute(value, lambda b, s, c: (b, s ^ (2 if c == 0 else 1), c))

    def send(value, k, m):
        return permute(value, lambda b, s, c: (b ^ k, s, (c + m) % narrow))

    def give_back(value, k, m):
        if k == 0 and m == 0:
            return value
        return permute(value, lambda b, s, c: (b ^ k, s, (c - m) % narrow))

    both_w = jnp.concatenate([w_gate[0], w_up[0]], axis=1)
    both_in = swap_weights(both_w)
    down_in = swap_weights(w_down[0])
    units = w_gate.shape[2]

    order = [blocks // 2] + [k for k in range(1, blocks) if k != blocks // 2] + [0]
    token = jnp.arange(count, dtype=jnp.int32)
    twins = (expert_ids[:, None] == expert_ids[None, :]) & (token[:, None] < token[None, :])
    slot = jnp.sum(twins.astype(jnp.int32), axis=0)
    shift = (expert_ids % blocks) ^ block
    position = sum(i * (shift == k).astype(jnp.int32) for i, k in enumerate(order))
    turn = (expert_ids // blocks - core + narrow) % narrow
    place = (position * narrow + turn) * cap + slot
    select = jnp.arange(experts * cap, dtype=jnp.int32)[:, None] == place[None, :]
    packed_x = times(select.astype(jnp.bfloat16), tokens).astype(jnp.bfloat16)
    packed_g = times(select.astype(jnp.bfloat16), grad_out).astype(jnp.bfloat16)
    packed = jnp.stack(
        [
            packed_x.reshape(blocks, narrow, cap, width),
            packed_g.reshape(blocks, narrow, cap, width),
        ],
        axis=2,
    )

    turned = [
        permute(packed[:, m], lambda b, s, c: (b, s, (c + m) % narrow)) for m in range(1, narrow)
    ]
    merged = jnp.stack([packed[:, 0]] + turned, axis=1)
    arrived = []
    for i, k in enumerate(order):
        if k == 0:
            arrived.append(merged[i])
        else:
            chunk = merged[i] if i < 2 else tie(merged[i], arrived[i - 2])
            arrived.append(send(chunk, k, 0))

    swapped = [None] * blocks

    def swap_in(i, *wait):
        swapped[i] = swap_rows(tie(arrived[i], *wait))

    def compute(i, *wait):
        mine, other = arrived[i], tie(swapped[i], *wait)
        x = jnp.concatenate([mine[:, 0].reshape(half, width), other[:, 0].reshape(half, width)])
        g = jnp.concatenate([mine[:, 1].reshape(half, width), other[:, 1].reshape(half, width)])
        partial, prob = 0.0, 0.0
        for forward_w, down_w in ((both_w, w_down[0]), (both_in, down_in)):
            forward = times(x, forward_w)
            gate, up = forward[:, :units], forward[:, units:]
            back = times_transposed(g, down_w)
            act, slope = silu_parts(gate)
            prob = prob + jnp.sum(act * up * back, axis=1)
            grads = jnp.concatenate([back * up * slope, back * act], axis=1).astype(jnp.bfloat16)
            partial = partial + times_transposed(grads, forward_w)
        theirs = with_prob(partial[half:], prob[half:])
        return partial[:half], prob[:half], theirs

    def finish(i, part, *wait):
        partial, prob, theirs = part
        theirs = tie(swap_rows(theirs), *wait).astype(jnp.float32)
        total = with_prob(
            partial + theirs[:, :width], prob + (theirs[:, width] + theirs[:, width + 1])
        )
        return total

    parts = [None] * blocks
    totals = [None] * blocks
    swap_in(0)
    swap_in(1)
    for i in range(blocks):
        last = i == blocks - 1
        if i > 1:
            swap_in(i, parts[i - 1 if last else i - 2][2])
        if i == 0:
            wait = []
        elif i == 1 or last:
            wait = [totals[i - 1]]
        else:
            wait = [parts[i - 1][2]]
        parts[i] = compute(i, *wait)
        if i == 0:
            totals[i] = finish(i, parts[i], *arrived[2:3])
        if i > 1 and not last:
            totals[i - 1] = finish(i - 1, parts[i - 1], parts[i][2])
        if i > 0 and i >= blocks - 2:
            totals[i] = finish(i, parts[i])

    rows = 0.0
    select = select.T.reshape(count, blocks, half).astype(jnp.bfloat16)
    for i in range(blocks):
        total = totals[i] if order[i] == 0 else give_back(totals[i], order[i], 0)
        parts_in = [total[:cap]]
        for m in range(1, narrow):
            parts_in.append(give_back(total[m * cap : (m + 1) * cap], 0, m))
        rows = rows + times(select[:, i], jnp.concatenate(parts_in, axis=0))
    token_grad = (combine[:, None] * rows[:, :width]).astype(jnp.bfloat16)
    prob_grad = rows[:, width] + rows[:, width + 1]
    return (token_grad, prob_grad)


def solution(mesh):
    in_specs = (
        P(("parts", "wide", "narrow"), None),
        P(("parts", "wide", "narrow"), None),
        P(("parts", "wide", "narrow")),
        P(("parts", "wide", "narrow")),
        P("narrow", None, "wide"),
        P("narrow", None, "wide"),
        P("narrow", "wide", None),
    )
    out_specs = (P(("parts", "wide", "narrow"), None), P(("parts", "wide", "narrow")))
    return jax.shard_map(shards, mesh=mesh, in_specs=in_specs, out_specs=out_specs, check_vma=False)
```

```python
import functools

import jax
import jax.numpy as jnp
from jax import lax
from jax.experimental import pallas as pl
from jax.experimental.pallas import tpu as pltpu
from jax.sharding import PartitionSpec as P

SHARDS = 4
LANES = 128
AXES = ("wide", "narrow")


def silu_parts(gate):
    sigma = jax.nn.sigmoid(gate)
    return (gate * sigma, sigma * (1.0 + gate * (1.0 - sigma)))


def times(left, right):
    return jnp.dot(left, right, preferred_element_type=jnp.float32)


def times_transposed(left, right):
    return lax.dot_general(
        left, right, (((1,), (1,)), ((), ())), preferred_element_type=jnp.float32
    )


def tie(value, *before):
    return lax.optimization_barrier((value,) + before)[0]


def with_prob(rows, prob):
    high = lax.reduce_precision(prob, 8, 7)
    column = lax.broadcasted_iota(jnp.int32, (prob.shape[0], LANES), 1)
    tail = jnp.where(
        column == 0, high[:, None], jnp.where(column == 1, (prob - high)[:, None], 0.0)
    )
    return jnp.concatenate([rows.astype(jnp.bfloat16), tail.astype(jnp.bfloat16)], axis=1)


def gather_rows(mine, other, x, g):
    sources, _, cap, _ = mine.shape
    for j in range(sources):
        for k, ref in ((0, mine), (1, other)):
            rows = slice((k * sources + j) * cap, (k * sources + j + 1) * cap)
            x[rows, :] = ref[j, 0]
            g[rows, :] = ref[j, 1]


def forward_and_grads(x, g, pairs, grads):
    total = 0.0
    for i, (two, one) in enumerate(pairs):
        units = one.shape[0]
        forward = times(x[...], two[...])
        ret = times_transposed(g[...], one[...])
        gate, up = forward[:, :units], forward[:, units:]
        act, slope = silu_parts(gate)
        total += jnp.sum(act * up * ret, axis=1, keepdims=True)
        grads[i, :, :units] = (ret * up * slope).astype(jnp.bfloat16)
        grads[i, :, units:] = (ret * act).astype(jnp.bfloat16)
    return total


def first_kernel(mine, other, both, down, sums, probs, x, g, grads):
    gather_rows(mine, other, x, g)
    total = forward_and_grads(x, g, ((both, down),), grads)
    sums[...] = times_transposed(grads[0], both[...])
    probs[...] = jnp.broadcast_to(total, probs.shape)


def last_kernel(before, *refs):
    mine, other, refs = refs[0], refs[1], refs[2:]
    if before:
        sums, probs, refs = refs[0], refs[1], refs[2:]
    *weights, part, prob, theirs, x, g, grads = refs
    pairs = tuple(zip(weights[::2], weights[1::2]))
    half, width = part.shape
    gather_rows(mine, other, x, g)
    total = forward_and_grads(x, g, pairs, grads)
    out = sums[...] if before else 0.0
    for i, (two, _) in enumerate(pairs):
        out += times_transposed(grads[i], two[...])
    if before:
        total += probs[:, :1]
    part[...] = out[:half]
    theirs[:, :width] = out[half:].astype(jnp.bfloat16)
    prob[...] = jnp.broadcast_to(total[:half], prob.shape)
    high = total[half:].astype(jnp.bfloat16).astype(jnp.float32)
    column = lax.broadcasted_iota(jnp.int32, (half, LANES), 1)
    tail = jnp.where(column == 0, high, jnp.where(column == 1, total[half:] - high, 0.0))
    theirs[:, width:] = tail.astype(jnp.bfloat16)


def call(kernel, out_shape, mine, operands, count, name):
    sources, _, cap, width = mine.shape
    rows, units = 2 * sources * cap, operands[-1].shape[0]
    vmem = pl.BlockSpec(memory_space=pltpu.VMEM)
    return pl.pallas_call(
        kernel,
        out_shape=out_shape,
        in_specs=[vmem] * (1 + len(operands)),
        out_specs=(vmem,) * len(out_shape),
        scratch_shapes=[
            pltpu.VMEM((rows, width), jnp.bfloat16),
            pltpu.VMEM((rows, width), jnp.bfloat16),
            pltpu.VMEM((count, rows, 2 * units), jnp.bfloat16),
        ],
        compiler_params=pltpu.CompilerParams(vmem_limit_bytes=28 * 2**20),
        cost_estimate=pl.CostEstimate(
            flops=2000000001 * count, bytes_accessed=1, transcendentals=0
        ),
        name=name,
    )(mine, *operands)


def first_sums(mine, other, both_w, down_w):
    rows, width = 2 * mine.shape[0] * mine.shape[2], mine.shape[3]
    out_shape = (
        jax.ShapeDtypeStruct((rows, width), jnp.float32),
        jax.ShapeDtypeStruct((rows, LANES), jnp.float32),
    )
    return call(first_kernel, out_shape, mine, (other, both_w, down_w), 1, "first_sums")


def chunk_sums(mine, other, *operands):
    before = operands[0].dtype == jnp.float32
    half, width = mine.shape[0] * mine.shape[2], mine.shape[3]
    out_shape = (
        jax.ShapeDtypeStruct((half, width), jnp.float32),
        jax.ShapeDtypeStruct((half, LANES), jnp.float32),
        jax.ShapeDtypeStruct((half, width + LANES), jnp.bfloat16),
    )
    kernel = functools.partial(last_kernel, before)
    count = len(operands) // 2 - int(before)
    return call(kernel, out_shape, mine, (other,) + operands, count, "chunk_sums")


def shards(tokens, grad_out, expert_ids, combine, w_gate, w_up, w_down):
    wide = lax.axis_size("wide")
    narrow = lax.axis_size("narrow")
    blocks = wide // SHARDS
    experts = blocks * narrow
    count, width = tokens.shape
    cap = 2 * count // experts
    half = narrow * cap
    block = lax.axis_index("wide") // SHARDS
    core = lax.axis_index("narrow")

    def permute(value, target):
        pairs = []
        for w in range(wide):
            for c in range(narrow):
                b, s, n = target(w // SHARDS, w % SHARDS, c)
                pairs.append((w * narrow + c, (b * SHARDS + s) * narrow + n))
        return lax.ppermute(value, AXES, pairs)

    def swap_weights(value):
        return permute(value, lambda b, s, c: (b, s ^ (1 if c == 0 else 2), c))

    def swap_rows(value):
        return permute(value, lambda b, s, c: (b, s ^ (2 if c == 0 else 1), c))

    def send(value, k, m):
        return permute(value, lambda b, s, c: (b ^ k, s, (c + m) % narrow))

    def give_back(value, k, m):
        if k == 0 and m == 0:
            return value
        return permute(value, lambda b, s, c: (b ^ k, s, (c - m) % narrow))

    both_w = jnp.concatenate([w_gate[0], w_up[0]], axis=1)
    both_in = swap_weights(both_w)
    down_in = swap_weights(w_down[0])
    units = w_gate.shape[2]

    order = [blocks // 2] + [k for k in range(1, blocks) if k != blocks // 2] + [0]
    token = jnp.arange(count, dtype=jnp.int32)
    twins = (expert_ids[:, None] == expert_ids[None, :]) & (token[:, None] < token[None, :])
    slot = jnp.sum(twins.astype(jnp.int32), axis=0)
    shift = (expert_ids % blocks) ^ block
    position = sum(i * (shift == k).astype(jnp.int32) for i, k in enumerate(order))
    turn = (expert_ids // blocks - core + narrow) % narrow
    place = (position * narrow + turn) * cap + slot
    select = jnp.arange(experts * cap, dtype=jnp.int32)[:, None] == place[None, :]
    packed_x = times(select.astype(jnp.bfloat16), tokens).astype(jnp.bfloat16)
    packed_g = times(select.astype(jnp.bfloat16), grad_out).astype(jnp.bfloat16)
    packed = jnp.stack(
        [
            packed_x.reshape(blocks, narrow, cap, width),
            packed_g.reshape(blocks, narrow, cap, width),
        ],
        axis=2,
    )

    turned = [
        permute(packed[:, m], lambda b, s, c: (b, s, (c + m) % narrow)) for m in range(1, narrow)
    ]
    merged = jnp.stack([packed[:, 0]] + turned, axis=1)
    arrived = []
    for i, k in enumerate(order):
        if k == 0:
            arrived.append(merged[i])
        else:
            chunk = merged[i] if i < 2 else tie(merged[i], arrived[0])
            arrived.append(send(chunk, k, 0))

    swapped = [None] * blocks

    def swap_in(i, *wait):
        swapped[i] = swap_rows(tie(arrived[i], *wait))

    def compute(i, *wait):
        mine, other = arrived[i], tie(swapped[i], *wait)
        if cap % 16:
            mine, other = (
                value.swapaxes(0, 1).reshape(1, 2, half, width) for value in (mine, other)
            )
        if i == 0:
            sums = first_sums(mine, other, both_w, w_down[0])
            part, prob, theirs = chunk_sums(mine, other, *sums, both_in, down_in)
        else:
            part, prob, theirs = chunk_sums(mine, other, both_w, w_down[0], both_in, down_in)
        return part, prob[:, 0], theirs

    def finish(i, part, *wait):
        partial, prob, theirs = part
        theirs = tie(swap_rows(theirs), *wait).astype(jnp.float32)
        total = with_prob(
            partial + theirs[:, :width], prob + (theirs[:, width] + theirs[:, width + 1])
        )
        return total

    own = blocks - 1
    final = own - 1
    parts = [None] * blocks
    totals = [None] * blocks
    swap_in(0, arrived[1])
    swap_in(1)
    parts[0] = compute(0)
    totals[0] = finish(0, parts[0], arrived[2], swapped[1])
    for i in range(1, final):
        parts[i] = compute(i, totals[i - 1])
        swap_in(i + 1, parts[i - 1][2])
        if i + 1 < final:
            totals[i] = finish(i, parts[i])
    parts[final] = compute(final, parts[final - 1][2])
    totals[final - 1] = finish(final - 1, parts[final - 1], parts[final][2])
    totals[final] = finish(final, parts[final])
    swap_in(own, parts[final][2])
    parts[own] = compute(own, totals[final])
    totals[own] = finish(own, parts[own])

    select = select.T.reshape(count, blocks, half).astype(jnp.bfloat16)
    rows = 0.0
    for i in range(blocks):
        total = totals[i] if order[i] == 0 else give_back(totals[i], order[i], 0)
        parts_in = [total[:cap]]
        for m in range(1, narrow):
            piece = total[m * cap : (m + 1) * cap]
            parts_in.append(give_back(piece, 0, m))
        rows = rows + times(select[:, i], jnp.concatenate(parts_in, axis=0))
    token_grad = (combine[:, None] * rows[:, :width]).astype(jnp.bfloat16)
    prob_grad = rows[:, width] + rows[:, width + 1]
    return (token_grad, prob_grad)


def solution(mesh):
    in_specs = (
        P(("parts", "wide", "narrow"), None),
        P(("parts", "wide", "narrow"), None),
        P(("parts", "wide", "narrow")),
        P(("parts", "wide", "narrow")),
        P("narrow", None, "wide"),
        P("narrow", None, "wide"),
        P("narrow", "wide", None),
    )
    out_specs = (P(("parts", "wide", "narrow"), None), P(("parts", "wide", "narrow")))
    return jax.shard_map(shards, mesh=mesh, in_specs=in_specs, out_specs=out_specs, check_vma=False)
```

```python
import jax
import jax.numpy as jnp
from jax import lax
from jax.sharding import PartitionSpec as P

SHARDS = 4
LANES = 128
AXES = ("wide", "narrow")


def silu_parts(gate):
    sigma = jax.nn.sigmoid(gate)
    return (gate * sigma, sigma * (1.0 + gate * (1.0 - sigma)))


def times(left, right):
    return jnp.dot(left, right, preferred_element_type=jnp.float32)


def times_transposed(left, right):
    return lax.dot_general(
        left, right, (((1,), (1,)), ((), ())), preferred_element_type=jnp.float32
    )


def tie(value, *before):
    return lax.optimization_barrier((value,) + before)[0]


def with_prob(rows, prob):
    high = lax.reduce_precision(prob, 8, 7)
    column = lax.broadcasted_iota(jnp.int32, (prob.shape[0], LANES), 1)
    tail = jnp.where(
        column == 0, high[:, None], jnp.where(column == 1, (prob - high)[:, None], 0.0)
    )
    return jnp.concatenate([rows.astype(jnp.bfloat16), tail.astype(jnp.bfloat16)], axis=1)


def shards(tokens, grad_out, expert_ids, combine, w_gate, w_up, w_down):
    wide = lax.axis_size("wide")
    narrow = lax.axis_size("narrow")
    blocks = wide // SHARDS
    experts = blocks * narrow
    count, width = tokens.shape
    cap = 2 * count // experts
    half = narrow * cap
    block = lax.axis_index("wide") // SHARDS
    core = lax.axis_index("narrow")

    def permute(value, target):
        pairs = []
        for w in range(wide):
            for c in range(narrow):
                b, s, n = target(w // SHARDS, w % SHARDS, c)
                pairs.append((w * narrow + c, (b * SHARDS + s) * narrow + n))
        return lax.ppermute(value, AXES, pairs)

    def swap_weights(value):
        return permute(value, lambda b, s, c: (b, s ^ (1 if c == 0 else 2), c))

    def swap_rows(value):
        return permute(value, lambda b, s, c: (b, s ^ (2 if c == 0 else 1), c))

    def send(value, k, m):
        return permute(value, lambda b, s, c: (b ^ k, s, (c + m) % narrow))

    def give_back(value, k, m):
        if k == 0 and m == 0:
            return value
        return permute(value, lambda b, s, c: (b ^ k, s, (c - m) % narrow))

    both_w = jnp.concatenate([w_gate[0], w_up[0]], axis=1)
    both_in = swap_weights(both_w)
    down_in = swap_weights(w_down[0])
    units = w_gate.shape[2]

    order = [blocks // 2] + [k for k in range(1, blocks) if k != blocks // 2] + [0]
    token = jnp.arange(count, dtype=jnp.int32)
    twins = (expert_ids[:, None] == expert_ids[None, :]) & (token[:, None] < token[None, :])
    slot = jnp.sum(twins.astype(jnp.int32), axis=0)
    shift = (expert_ids % blocks) ^ block
    position = sum(i * (shift == k).astype(jnp.int32) for i, k in enumerate(order))
    turn = (expert_ids // blocks - core + narrow) % narrow
    place = (position * narrow + turn) * cap + slot
    select = jnp.arange(experts * cap, dtype=jnp.int32)[:, None] == place[None, :]
    packed_x = times(select.astype(jnp.bfloat16), tokens).astype(jnp.bfloat16)
    packed_g = times(select.astype(jnp.bfloat16), grad_out).astype(jnp.bfloat16)
    packed = jnp.stack(
        [
            packed_x.reshape(blocks, narrow, cap, width),
            packed_g.reshape(blocks, narrow, cap, width),
        ],
        axis=2,
    )

    merged = []
    for lot in (slice(0, 2), slice(2, blocks)):
        turned = [
            permute(packed[lot, m], lambda b, s, c: (b, s, (c + m) % narrow))
            for m in range(1, narrow)
        ]
        lots = jnp.stack([packed[lot, 0]] + turned, axis=1)
        merged += [lots[i] for i in range(lots.shape[0])]
    arrived = []
    for i, k in enumerate(order):
        if k == 0:
            arrived.append(merged[i])
        else:
            chunk = merged[i] if i < 2 else tie(merged[i], arrived[i - 2])
            arrived.append(send(chunk, k, 0))

    swapped = [None] * blocks

    def swap_in(i, *wait):
        swapped[i] = swap_rows(tie(arrived[i], *wait))

    def compute(i, *wait):
        mine, other = arrived[i], tie(swapped[i], *wait)
        x = jnp.concatenate([mine[:, 0].reshape(half, width), other[:, 0].reshape(half, width)])
        g = jnp.concatenate([mine[:, 1].reshape(half, width), other[:, 1].reshape(half, width)])
        partial, prob = 0.0, 0.0
        for forward_w, down_w in ((both_w, w_down[0]), (both_in, down_in)):
            forward = times(x, forward_w)
            gate, up = forward[:, :units], forward[:, units:]
            back = times_transposed(g, down_w)
            act, slope = silu_parts(gate)
            prob = prob + jnp.sum(act * up * back, axis=1)
            grads = jnp.concatenate([back * up * slope, back * act], axis=1).astype(jnp.bfloat16)
            partial = partial + times_transposed(grads, forward_w)
        theirs = with_prob(partial[half:], prob[half:])
        return partial[:half], prob[:half], theirs

    def finish(i, part, *wait):
        partial, prob, theirs = part
        theirs = tie(swap_rows(theirs), *wait).astype(jnp.float32)
        total = with_prob(
            partial + theirs[:, :width], prob + (theirs[:, width] + theirs[:, width + 1])
        )
        return total

    parts = [None] * blocks
    totals = [None] * blocks
    swap_in(0)
    swap_in(1)
    for i in range(blocks):
        last = i == blocks - 1
        if i > 1:
            swap_in(i, parts[i - 1 if last else i - 2][2])
        if i == 0:
            wait = []
        elif i == 1 or last:
            wait = [totals[i - 1]]
        else:
            wait = [parts[i - 1][2]]
        parts[i] = compute(i, *wait)
        if i == 0:
            totals[i] = finish(i, parts[i], *arrived[2:3])
        if i > 1 and not last:
            totals[i - 1] = finish(i - 1, parts[i - 1], parts[i][2])
        if i > 0 and i >= blocks - 2:
            totals[i] = finish(i, parts[i])

    rows = 0.0
    select = select.T.reshape(count, blocks, half).astype(jnp.bfloat16)
    for i in range(blocks):
        total = totals[i] if order[i] == 0 else give_back(totals[i], order[i], 0)
        parts_in = [total[:cap]]
        for m in range(1, narrow):
            parts_in.append(give_back(total[m * cap : (m + 1) * cap], 0, m))
        rows = rows + times(select[:, i], jnp.concatenate(parts_in, axis=0))
    token_grad = (combine[:, None] * rows[:, :width]).astype(jnp.bfloat16)
    prob_grad = rows[:, width] + rows[:, width + 1]
    return (token_grad, prob_grad)


def solution(mesh):
    in_specs = (
        P(("parts", "wide", "narrow"), None),
        P(("parts", "wide", "narrow"), None),
        P(("parts", "wide", "narrow")),
        P(("parts", "wide", "narrow")),
        P("narrow", None, "wide"),
        P("narrow", None, "wide"),
        P("narrow", "wide", None),
    )
    out_specs = (P(("parts", "wide", "narrow"), None), P(("parts", "wide", "narrow")))
    return jax.shard_map(shards, mesh=mesh, in_specs=in_specs, out_specs=out_specs, check_vma=False)
```
